32 devices in a mesh: req: 8 (over z, y), exp: 4 (over x, core).
Axes of the slice: x: 2, y: 2, z: 4, core: 2. Of those that a mesh axis runs over, the one named last changes fastest.
Arguments:
- residual: bfloat16 [4096, 2048], P(('req', 'exp')), may hold values from -3 to 3
- query_vectors: bfloat16 [4096, 2048], P(('req', 'exp')), may hold values from -12 to 12
- key_vectors: bfloat16 [4096, 2048], P(('req', 'exp')), may hold values from -12 to 12
- value_vectors: bfloat16 [4096, 2048], P(('req', 'exp')), may hold values from -6 to 6
- segment_ids: int32 [4096], P('req'), may hold values from 0 to 2, as said below
- prompt_lengths: int32 [8, 3], replicated, may hold values from 1 to 256, as said below
- request_groups: int32 [8], replicated, may hold values from 0 to 7, as said below
- page_table: int32 [8, 4], replicated, may hold values from 0 to 31, as said below
- expert_ids: int32 [4096, 8], P(('req', 'exp')), may hold values from 0 to 15, all different within a row; in each aligned block of 128 rows (0 to 127, 128 to 255, ...) at most 96 rows name the same one
- gate_weights: float32 [4096, 8], P(('req', 'exp')), may hold values from 0.1 to 0.6
- out_weight: bfloat16 [2048, 2048], replicated, may hold values from -0.125 to 0.125
- norm_gain: float32 [2048], replicated, may hold values from 0.5 to 2
- expert_inner: bfloat16 [32, 2048, 1024], P(('req', 'exp')), may hold values from -0.125 to 0.125
- expert_outer: bfloat16 [32, 512, 2048], P(('req', 'exp')), may hold values from -0.1875 to 0.1875
Outputs:
- layer_out: bfloat16 [4096, 2048], P(('req', 'exp'))
- kv_pages: bfloat16 [32, 2, 128, 2048], P('req', None, None, 'exp')
The draws below stay inside these ranges and needn't reach their ends.
Inputs may be any that keep to these rules, and one draw needn't show every extreme that they name: `prompt_lengths`: each row sums to 512, and its largest entry is 256. `segment_ids`: within each group of 512 rows the numbers never fall; prompt j of the request r with request_groups[r] = g fills prompt_lengths[r, j] consecutive rows of group g. `request_groups`: each group appears once. `page_table`: all entries differ; the 4 pages of one request lie in 4 different owner groups, the owner of slot s being s // 4. `expert_ids`: the 8 ids of a token differ; among the 128 tokens of one device no expert is named more than 96 times, a bound that some block reaches.
All inputs are finite; a program needn't handle non-finite values.
Results may differ from the reference program's by a relative error of at most 0.013.
Values may be sent and summed in bfloat16 or wider, within the bound.
A program may use at most 192 MiB of HBM per device.

```python
import math
import jax
import jax.numpy as jnp
import numpy as np
from jax import lax

D = 2048
HEADS = 16
HEAD = 128
FF = 1024
TOP = 8
TOK_DEV = 128
PAGE = 128
SEGS = 3
HD = 2048
EXPERTS = 16
TOK_GRP = 512
TOKENS = 4096
PAGES_REQ = 4
SLOTS = 32
PROMPT_MAX = 256
CAP = 96
N_REQ = 8
DEVICES = 32


def request_layout(key):
    key_perm = jax.random.fold_in(key, 7001)
    key_longest = jax.random.fold_in(key, 7002)
    key_weight = jax.random.fold_in(key, 7003)
    key_offset = jax.random.fold_in(key, 7004)
    key_local = jax.random.fold_in(key, 7005)
    groups_of = jax.random.permutation(key_perm, N_REQ).astype(jnp.int32)
    longest = jax.random.randint(key_longest, (N_REQ,), 0, SEGS)
    weights = jax.random.randint(key_weight, (N_REQ, SEGS), 1, 101)
    column = jnp.arange(SEGS)[None, :]
    is_longest = column == longest[:, None]
    weights = jnp.where(is_longest, 0, weights)
    spare_tokens = TOK_GRP - PROMPT_MAX - (SEGS - 1)
    shares = spare_tokens * weights // jnp.sum(weights, axis=1, keepdims=True)
    leftover = spare_tokens - jnp.sum(shares, axis=1, keepdims=True)
    extra_tokens = jnp.where(column == (longest[:, None] + 1) % SEGS, leftover, 0)
    group_lengths = jnp.where(is_longest, PROMPT_MAX, 1 + shares + extra_tokens).astype(jnp.int32)
    prompt_lengths = group_lengths[groups_of]
    prompt_ends = jnp.cumsum(group_lengths, axis=1)
    positions = jnp.arange(TOK_GRP)
    segment_ids = jnp.sum((positions[None, :, None] >= prompt_ends[:, None, :SEGS - 1]).astype(jnp.int32), axis=2).reshape(TOKENS)
    offsets = jax.random.permutation(key_offset, N_REQ)[:PAGES_REQ]
    owners = (jnp.arange(N_REQ)[:, None] + offsets[None, :]) % N_REQ
    local_keys = jax.random.split(key_local, N_REQ)
    local_order = jax.vmap(lambda one_key: jax.random.permutation(one_key, PAGES_REQ))(local_keys)
    local_slot = local_order[owners, jnp.arange(PAGES_REQ)[None, :]]
    page_table = (owners * PAGES_REQ + local_slot).astype(jnp.int32)
    return (groups_of, prompt_lengths.astype(jnp.int32), segment_ids.astype(jnp.int32), page_table)


def draw_request_groups(key, part):
    return request_layout(key)[0]


def draw_prompt_lengths(key, part):
    return request_layout(key)[1]


def draw_segment_ids(key, part):
    return request_layout(key)[2]


def draw_page_table(key, part):
    return request_layout(key)[3]


def query_key_pair(key):
    key_query = jax.random.fold_in(key, 8101)
    key_key = jax.random.fold_in(key, 8102)
    queries = 1.3 * jax.random.normal(key_query, (TOKENS, HD))
    keys = 1.3 * jax.random.normal(key_key, (TOKENS, HD))
    return (jnp.clip(queries, -12.0, 12.0).astype(jnp.float32), jnp.clip(keys, -12.0, 12.0).astype(jnp.float32))


def draw_query_vectors(key, part):
    return query_key_pair(key)[0].astype(jnp.bfloat16)


def draw_key_vectors(key, part):
    return query_key_pair(key)[1].astype(jnp.bfloat16)


def steps_of(stream_key, dims, cuts, least, high):
    def one(axis_at, shards_of):
        draws = jax.random.uniform(jax.random.fold_in(jax.random.fold_in(stream_key, 6), axis_at), (shards_of,), jnp.float32, least / len(cuts), high / len(cuts))
        return jnp.repeat(jnp.exp(draws), dims[axis_at] // shards_of).reshape((-1,) + (1,) * (len(dims) - axis_at - 1))

    level = one(*cuts[0])
    for cut in cuts[1:]:
        level = level * one(*cut)
    return level


def assign_block(stream_key, own, number, rows, count, top, limit, slope):
    sequence = jax.random.permutation(stream_key, count)
    heavy_load, ordinary = portions_of(count, rows * top, limit, slope, True), portions_of(count, rows * top, limit, slope, False)
    places = jnp.arange(count)

    def named(sizes, rotation):
        used = int((sizes > 0).sum())
        fixed = max(1, used // 4)
        shifted = fixed + (places - fixed + rotation * (used - fixed)) % max(1, count - fixed)
        return jnp.zeros((count,), jnp.int32).at[sequence[jnp.where(places < fixed, places, shifted)]].set(jnp.asarray(sizes, jnp.int32))

    sizes = jnp.where(number % 4 == 0, named(heavy_load, number // 4), named(ordinary, number - number // 4 - 1))
    mixed = jax.random.permutation(jax.random.fold_in(own, 3), count)
    donor, receiver = mixed[0:count // 2 * 2:2], mixed[1:count // 2 * 2:2]
    room = jnp.minimum(sizes[donor] - 1, limit - sizes[receiver]) // 2
    room = jnp.where((donor == sequence[0]) | (receiver == sequence[0]) | (sizes[receiver] == 0), 0, jnp.maximum(room, 0))
    shifted = jax.random.randint(jax.random.fold_in(own, 4), (count // 2,), 0, 1 << 20) % (room + 1)
    sizes = sizes.at[donor].add(-shifted).at[receiver].add(shifted)
    labels = jnp.searchsorted(jnp.cumsum(sizes), jnp.arange(rows * top), side="right").astype(jnp.int32)
    grid = labels.reshape(top, rows).T
    grid = grid[jax.random.permutation(jax.random.fold_in(own, 1), rows)]
    rotation = jax.random.randint(jax.random.fold_in(own, 2), (rows, 1), 0, top)
    return jnp.take_along_axis(grid, (jnp.arange(top)[None, :] + rotation) % top, axis=1)


def portions_of(count, total, reach, slope, full):
    weights = [(1 << 20) // math.isqrt(grade ** slope) + 1 for grade in range(1, count + 1)]
    largest = reach if full else min(reach, max(-(-total // count), total * weights[0] // sum(weights)))
    least = 1 if total - largest >= count - 1 else 0
    given, surplus = [largest] + [least] * (count - 1), total - largest - least * (count - 1)
    while surplus > 0:
        movable = [i for i in range(1, count) if given[i] < largest] or [i for i in range(1, count) if given[i] < reach]
        whole, budget = sum([weights[i] for i in movable]), surplus
        for i in movable:
            addition = min(reach - given[i], max(1, budget * weights[i] // whole), surplus)
            given[i] = given[i] + addition
            surplus = surplus - addition
    return np.array(given)


def noise(rng, shape, width, limit, shards=(), held_as=jnp.bfloat16):
    values = width * jax.random.normal(rng, shape, jnp.float32)
    if shards:
        values = values * steps_of(rng, shape, shards, -0.22, 0.18)
    return jnp.clip(values, -limit, limit).astype(held_as)


def setup_inputs(seed: int = 0) -> dict:
    arg_keys = jax.random.split(jax.random.key(seed), 15)
    residual = noise(arg_keys[0], (TOKENS, D), 0.5, 3.0, ((0, 32),))
    query_vectors = draw_query_vectors(jax.random.fold_in(arg_keys[14], 71), 0)
    key_vectors = draw_key_vectors(jax.random.fold_in(arg_keys[14], 71), 0)
    value_vectors = noise(arg_keys[3], (TOKENS, HD), 1.0, 6.0, ((0, 32),))
    segment_ids = draw_segment_ids(jax.random.fold_in(arg_keys[14], 71), 0)
    prompt_lengths = draw_prompt_lengths(jax.random.fold_in(arg_keys[14], 71), 0)
    request_groups = draw_request_groups(jax.random.fold_in(arg_keys[14], 71), 0)
    page_table = draw_page_table(jax.random.fold_in(arg_keys[14], 71), 0)
    expert_ids_keys = jax.random.split(jax.random.fold_in(arg_keys[8], 1), TOKENS // TOK_DEV)
    expert_ids_turns = jax.random.permutation(jax.random.fold_in(arg_keys[8], 3), TOKENS // TOK_DEV)
    expert_ids = jax.vmap(lambda own, number: assign_block(jax.random.fold_in(arg_keys[8], 2), own, number, TOK_DEV, EXPERTS, TOP, CAP, 2))(expert_ids_keys, expert_ids_turns).reshape((TOKENS, TOP))
    gate_weights = jnp.clip(jnp.exp(math.log(0.6) - 1.7917595 * jax.random.uniform(arg_keys[9], (TOKENS, TOP), jnp.float32) ** steps_of(arg_keys[9], (TOKENS, TOP), ((0, 32),), -0.2, 0.2)), 0.1, 0.6)
    out_weight = noise(arg_keys[10], (HD, D), HD ** -0.5, 0.125)
    norm_gain = jnp.clip(jnp.exp(jax.random.uniform(arg_keys[11], (D,), jnp.float32, math.log(0.5), math.log(2.0))), 0.5, 2.0)
    expert_inner = noise(arg_keys[12], (2 * EXPERTS, D, FF), D ** -0.5, 0.125, ((0, 32),))
    expert_outer = noise(arg_keys[13], (2 * EXPERTS, FF // 2, D), FF ** -0.5, 0.1875, ((0, 32),))
    return dict(residual=residual, query_vectors=query_vectors, key_vectors=key_vectors, value_vectors=value_vectors, segment_ids=segment_ids, prompt_lengths=prompt_lengths, request_groups=request_groups, page_table=page_table, expert_ids=expert_ids, gate_weights=gate_weights, out_weight=out_weight, norm_gain=norm_gain, expert_inner=expert_inner, expert_outer=expert_outer)


rope_base = 10000.0
norm_eps = 1e-06
masked_score = -1e+30

def rotate(values_in, positions):
    row_count = values_in.shape[0]
    half_head = HEAD // 2
    inverse = rope_base ** (-(2.0 * jnp.arange(half_head, dtype=jnp.float32)) / HEAD)
    angles = positions[:, None] * inverse[None, :]
    cosine = jnp.cos(angles)[:, None, :]
    sines = jnp.sin(angles)[:, None, :]
    shaped = values_in.astype(jnp.float32).reshape(row_count, -1, HEAD)
    first_half = shaped[..., :half_head]
    second_half = shaped[..., half_head:]
    turned = jnp.concatenate([first_half * cosine - second_half * sines, second_half * cosine + first_half * sines], axis=-1)
    return turned.reshape(row_count, -1).astype(jnp.bfloat16)

def group_attention(operands):
    query_rows, key_rows, value_rows, group_segments = operands
    scores = jnp.einsum('qhd,khd->hqk', query_rows.astype(jnp.float32), key_rows.astype(jnp.float32)) * HEAD ** (-0.5)
    same_prompt = (group_segments[:, None] == group_segments[None, :])[None]
    scores = jnp.where(same_prompt, scores, masked_score)
    top_score = lax.optimization_barrier(jnp.max(scores, axis=-1, keepdims=True))
    weights = jnp.where(same_prompt, jnp.exp(scores - top_score), 0.0)
    totals = lax.optimization_barrier(jnp.sum(weights, axis=-1))
    rounded = lax.optimization_barrier(weights.astype(jnp.bfloat16))
    mixed = jnp.einsum('hqk,khd->qhd', rounded.astype(jnp.float32), value_rows.astype(jnp.float32))
    return (mixed / totals.T[:, :, None]).astype(jnp.bfloat16).reshape(TOK_GRP, HD)

def reference(residual, query_vectors, key_vectors, value_vectors, segment_ids, prompt_lengths, request_groups, page_table, expert_ids, gate_weights, out_weight, norm_gain, expert_inner, expert_outer):
    groups = jnp.arange(N_REQ, dtype=jnp.int32)
    holds_request = (request_groups[None, :] == groups[:, None]).astype(jnp.int32)
    group_lengths = lax.optimization_barrier(jnp.sum(holds_request[:, :, None] * prompt_lengths[None, :, :], axis=1))
    group_pages = lax.optimization_barrier(jnp.sum(holds_request[:, :, None] * page_table[None, :, :], axis=1))
    starts = jnp.cumsum(group_lengths, axis=1) - group_lengths
    segments = segment_ids.reshape(N_REQ, TOK_GRP)
    prompt_index = jnp.arange(prompt_lengths.shape[1], dtype=jnp.int32)
    token_start = lax.optimization_barrier(jnp.sum(jnp.where(segments[:, :, None] == prompt_index[None, None, :], starts[:, None, :], 0), axis=2))
    positions = (jnp.arange(TOK_GRP, dtype=jnp.int32)[None, :] - token_start).reshape(TOKENS).astype(jnp.float32)
    query_turned = rotate(query_vectors, positions)
    key_turned = rotate(key_vectors, positions)
    stacked = jnp.stack([key_turned.reshape(N_REQ * PAGES_REQ, PAGE, HD), value_vectors.reshape(N_REQ * PAGES_REQ, PAGE, HD)], axis=1)
    kv_pages = jnp.zeros((SLOTS, 2, PAGE, HD), jnp.bfloat16).at[group_pages.reshape(-1)].set(stacked)
    attention = lax.map(group_attention, (query_turned.reshape(N_REQ, TOK_GRP, HEADS, HEAD), key_turned.reshape(N_REQ, TOK_GRP, HEADS, HEAD), value_vectors.reshape(N_REQ, TOK_GRP, HEADS, HEAD), segments)).reshape(TOKENS, HD)
    hidden = residual.astype(jnp.float32) + jnp.dot(attention, out_weight, preferred_element_type=jnp.float32)
    normed = (hidden * lax.rsqrt(lax.optimization_barrier(jnp.mean(hidden * hidden, axis=-1, keepdims=True)) + norm_eps) * norm_gain).astype(jnp.bfloat16)
    expert_range = jnp.arange(EXPERTS, dtype=jnp.int32)
    chosen = (expert_ids[:, :, None] == expert_range[None, None, :]).astype(jnp.int32)
    picked = lax.optimization_barrier(jnp.sum(chosen, axis=1))
    earlier = jnp.cumsum(picked, axis=0) - picked
    expert_rank = lax.optimization_barrier(jnp.sum(chosen * earlier[:, None, :], axis=2))
    capacity_rows = DEVICES * CAP
    token_index = jnp.broadcast_to(jnp.arange(TOKENS, dtype=jnp.int32)[:, None], expert_ids.shape)
    slot_table = jnp.full((EXPERTS, capacity_rows), TOKENS, jnp.int32).at[expert_ids, expert_rank].set(token_index)
    padded = jnp.concatenate([normed, jnp.zeros((1, D), jnp.bfloat16)], axis=0)

    def expert_step(accumulated, operands):
        expert, inner_pair, outer_pair, slot_tokens = operands
        gathered = padded[slot_tokens]
        partial_sums = []
        for half_index in range(2):
            projected = jnp.dot(gathered, inner_pair[half_index], preferred_element_type=jnp.float32)
            half_units = projected.shape[1] // 2
            active = (jax.nn.silu(projected[:, :half_units]) * projected[:, half_units:]).astype(jnp.bfloat16)
            partial_sums.append(jnp.dot(active, outer_pair[half_index], preferred_element_type=jnp.float32))
        expert_out = (partial_sums[0] + partial_sums[1]).astype(jnp.bfloat16)
        weight_row = lax.optimization_barrier(jnp.sum(jnp.where(expert_ids == expert, gate_weights, 0.0), axis=1))
        weight_pad = jnp.concatenate([weight_row, jnp.zeros((1,), jnp.float32)])
        accumulated = accumulated.at[slot_tokens].add(weight_pad[slot_tokens][:, None] * expert_out.astype(jnp.float32))
        return (accumulated, None)
    accumulated, unused = lax.scan(expert_step, jnp.zeros((TOKENS + 1, D), jnp.float32), (expert_range, expert_inner.reshape(EXPERTS, 2, D, FF), expert_outer.reshape(EXPERTS, 2, FF // 2, D), slot_table))
    layer_out = (hidden + accumulated[:TOKENS]).astype(jnp.bfloat16)
    return (layer_out, kv_pages)
```

```python
import functools

import jax
import jax.numpy as jnp
from jax import lax
from jax.experimental import pallas as pl
from jax.experimental.pallas import tpu as pltpu
from jax.sharding import PartitionSpec as P

HEAD = 128
PAGE = 128

rope_base = 10000.0
norm_eps = 1e-06
masked_score = -1e30
CHUNKS = 2


def turn(block, cosine, sines):
    wide = block.astype(jnp.float32)
    return (wide * cosine + pltpu.roll(wide, HEAD // 2, 1) * sines).astype(jnp.bfloat16)


def turn_keys_kernel(key_ref, value_ref, cos_ref, sin_ref, out_ref):
    width = key_ref.shape[1]
    cosine, sines = cos_ref[...], sin_ref[...]
    for start in range(0, width, HEAD):
        out_ref[:, start : start + HEAD] = turn(
            key_ref[:, start : start + HEAD], cosine, sines
        )
    out_ref[:, width:] = value_ref[...]


def turn_keys(keys, values, cosine, sines):
    rows, width = keys.shape
    return pl.pallas_call(
        turn_keys_kernel,
        out_shape=jax.ShapeDtypeStruct((rows, 2 * width), jnp.bfloat16),
        compiler_params=pltpu.CompilerParams(vmem_limit_bytes=32 << 20),
        name="turn_keys",
    )(keys, values, cosine, sines)


def attention_kernel(query_ref, key_ref, value_ref, cos_ref, sin_ref, mine_ref, all_ref, out_ref):
    cosine, sines = cos_ref[...], sin_ref[...]
    same = mine_ref[...] == all_ref[...]
    for start in range(0, query_ref.shape[1], HEAD):
        cols = slice(start, start + HEAD)
        query = turn(query_ref[:, cols], cosine, sines)
        scores = lax.dot_general(
            query, key_ref[:, cols], (((1,), (1,)), ((), ())), preferred_element_type=jnp.float32
        ) * HEAD ** (-0.5)
        scores = jnp.where(same, scores, masked_score)
        weights = jnp.where(same, jnp.exp(scores - jnp.max(scores, axis=1, keepdims=True)), 0.0)
        totals = jnp.sum(weights, axis=1, keepdims=True)
        mixed = jnp.dot(
            weights.astype(jnp.bfloat16), value_ref[:, cols], preferred_element_type=jnp.float32
        )
        out_ref[:, cols] = (mixed / totals).astype(jnp.bfloat16)


def attend(queries, keys_values, cosine, sines, my_segments, segments):
    rows, width = queries.shape
    all_rows = keys_values.shape[0]
    step = 512
    steps = width // step
    return pl.pallas_call(
        attention_kernel,
        grid=(steps,),
        in_specs=[
            pl.BlockSpec((rows, step), lambda i: (0, i)),
            pl.BlockSpec((all_rows, step), lambda i: (0, i)),
            pl.BlockSpec((all_rows, step), lambda i: (0, i + steps)),
            pl.BlockSpec((rows, HEAD), lambda i: (0, 0)),
            pl.BlockSpec((rows, HEAD), lambda i: (0, 0)),
            pl.BlockSpec((rows, 1), lambda i: (0, 0)),
            pl.BlockSpec((1, all_rows), lambda i: (0, 0)),
        ],
        out_specs=pl.BlockSpec((rows, step), lambda i: (0, i)),
        out_shape=jax.ShapeDtypeStruct((rows, width), jnp.bfloat16),
        compiler_params=pltpu.CompilerParams(vmem_limit_bytes=32 << 20),
        name="attend",
    )(queries, keys_values, keys_values, cosine, sines, my_segments[:, None], segments[None, :])


def pack_kernel(index_ref, key_ref, value_ref, out_ref):
    out_ref[0, 0] = key_ref[0]
    out_ref[0, 1] = value_ref[0]


def pack_pages(pages, index, columns, member_count):
    count = index.shape[0] - 1
    return pl.pallas_call(
        pack_kernel,
        grid_spec=pltpu.PrefetchScalarGridSpec(
            num_scalar_prefetch=1,
            grid=(count,),
            in_specs=[
                pl.BlockSpec((1, PAGE, columns), lambda i, index: (index[i], 0, index[count])),
                pl.BlockSpec(
                    (1, PAGE, columns), lambda i, index: (index[i], 0, index[count] + member_count)
                ),
            ],
            out_specs=pl.BlockSpec((1, 2, PAGE, columns), lambda i, index: (i, 0, 0, 0)),
        ),
        out_shape=jax.ShapeDtypeStruct((count, 2, PAGE, columns), jnp.bfloat16),
        name="pack_pages",
    )(index, pages, pages)


def place_kernel(index_ref, in_ref, out_ref):
    out_ref[...] = in_ref[...]


def place_pages(incoming, index):
    block = (1,) + incoming.shape[1:]
    return pl.pallas_call(
        place_kernel,
        grid_spec=pltpu.PrefetchScalarGridSpec(
            num_scalar_prefetch=1,
            grid=index.shape,
            in_specs=[pl.BlockSpec(block, lambda i, index: (index[i], 0, 0, 0))],
            out_specs=pl.BlockSpec(block, lambda i, index: (i, 0, 0, 0)),
        ),
        out_shape=jax.ShapeDtypeStruct(index.shape + incoming.shape[1:], jnp.bfloat16),
        name="place_pages",
    )(index, incoming)


def expert_kernel(rows_ref, gate_ref, inner_ref, outer_ref, out_ref):
    projected = jnp.dot(rows_ref[...], inner_ref[0], preferred_element_type=jnp.float32)
    half = projected.shape[1] // 2
    first = projected[:, :half]
    active = (first / (1.0 + jnp.exp(-first)) * projected[:, half:]).astype(jnp.bfloat16)
    out = jnp.dot(active, outer_ref[0], preferred_element_type=jnp.float32)
    out_ref[...] = (out * gate_ref[...]).astype(jnp.bfloat16)


def half_expert(rows, gates, inner, outer):
    count, width = rows.shape
    step = min(512, count)
    once = pl.Buffered(1)
    return pl.pallas_call(
        expert_kernel,
        grid=(count // step,),
        in_specs=[
            pl.BlockSpec((step, width), lambda i: (i, 0)),
            pl.BlockSpec((step, 1), lambda i: (i, 0)),
            pl.BlockSpec(inner.shape, lambda i: (0, 0, 0), pipeline_mode=once),
            pl.BlockSpec(outer.shape, lambda i: (0, 0, 0), pipeline_mode=once),
        ],
        out_specs=pl.BlockSpec((step, width), lambda i: (i, 0)),
        out_shape=jax.ShapeDtypeStruct((count, width), jnp.bfloat16),
        compiler_params=pltpu.CompilerParams(vmem_limit_bytes=48 << 20),
        cost_estimate=pl.CostEstimate(
            flops=2 * count * width * (inner.shape[2] + outer.shape[1]),
            bytes_accessed=4 * count * width,
            transcendentals=0,
        ),
        name="half_expert",
    )(rows, gates, inner, outer)


def on_device(
    residual,
    query_vectors,
    key_vectors,
    value_vectors,
    segment_ids,
    prompt_lengths,
    request_groups,
    page_table,
    expert_ids,
    gate_weights,
    out_weight,
    norm_gain,
    expert_inner,
    expert_outer,
):
    tok_rows, model_width = residual.shape
    req_count = lax.axis_size("req")
    member_count = lax.axis_size("exp")
    device_count = req_count * member_count
    expert_count = device_count // 2
    group_rows = tok_rows * member_count
    page_count = group_rows // PAGE
    columns = model_width // member_count
    everyone = ("req", "exp")
    group = lax.axis_index("req")
    member = lax.axis_index("exp")
    expert = (group * member_count + member) // 2

    holds_request = (request_groups == group).astype(jnp.int32)
    my_lengths = jnp.sum(holds_request[:, None] * prompt_lengths, axis=0)
    my_pages = jnp.sum(holds_request[:, None] * page_table, axis=0)
    first_row = member * tok_rows
    my_segments = lax.dynamic_slice_in_dim(segment_ids, first_row, tok_rows, 0)
    prompt_index = jnp.arange(prompt_lengths.shape[1], dtype=jnp.int32)
    token_start = jnp.sum(
        jnp.where(prompt_index[None, :] < my_segments[:, None], my_lengths[None, :], 0), axis=1
    )
    positions = (first_row + jnp.arange(tok_rows, dtype=jnp.int32) - token_start).astype(
        jnp.float32
    )
    inverse = rope_base ** (-(2.0 * jnp.arange(HEAD // 2, dtype=jnp.float32)) / HEAD)
    angles = positions[:, None] * inverse[None, :]
    cosine, sines = jnp.cos(angles), jnp.sin(angles)
    cosine = jnp.concatenate([cosine, cosine], axis=1)
    sines = jnp.concatenate([-sines, sines], axis=1)

    mine = turn_keys(key_vectors, value_vectors, cosine, sines)
    keys_values = lax.all_gather(mine, "exp", axis=0, tiled=True)

    expert_range = jnp.arange(expert_count, dtype=jnp.int32)
    dense_gates = jnp.sum(
        jnp.where(
            expert_ids.T[None] == expert_range[:, None, None], gate_weights.T[None], 0.0
        ),
        axis=1,
    )
    all_gates = lax.all_gather(dense_gates, everyone, axis=0)
    my_gates = lax.dynamic_index_in_dim(all_gates, expert, 1, keepdims=False)

    group_range = jnp.arange(req_count, dtype=jnp.int32)
    page_range = jnp.arange(page_count, dtype=jnp.int32)
    owned = my_pages[None, :] // page_count == group_range[:, None]
    page_for_group = jnp.sum(jnp.where(owned, page_range[None, :], 0), axis=1)
    outgoing = pack_pages(
        keys_values.reshape(page_count, PAGE, 2 * model_width),
        jnp.concatenate([page_for_group, member[None]]).astype(jnp.int32),
        columns,
        member_count,
    )
    incoming = lax.all_to_all(outgoing, "req", split_axis=0, concat_axis=0, tiled=True)
    slot_ids = group * page_count + page_range
    holds_slot = jnp.any(page_table[None, :, :] == slot_ids[:, None, None], axis=2)
    source_of_slot = jnp.sum(jnp.where(holds_slot, request_groups[None, :], 0), axis=1)
    kv_pages = place_pages(incoming, source_of_slot.astype(jnp.int32))

    attention = attend(query_vectors, keys_values, cosine, sines, my_segments, segment_ids)
    hidden = residual.astype(jnp.float32) + jnp.dot(
        attention, out_weight, preferred_element_type=jnp.float32
    )
    normed = (
        hidden * lax.rsqrt(jnp.mean(hidden * hidden, axis=-1, keepdims=True) + norm_eps) * norm_gain
    ).astype(jnp.bfloat16)

    part = tok_rows // CHUNKS
    sums = []
    for chunk in range(CHUNKS):
        rows = slice(chunk * part, (chunk + 1) * part)
        gathered = lax.all_gather(normed[rows], everyone, axis=0, tiled=True)
        gates = my_gates[:, rows].reshape(-1, 1)
        partial_out = half_expert(gathered, gates, expert_inner, expert_outer)
        summed = lax.psum_scatter(partial_out, everyone, scatter_dimension=0, tiled=True)
        sums.append(hidden[rows] + summed.astype(jnp.float32))
    layer_out = jnp.concatenate(sums, axis=0).astype(jnp.bfloat16)
    return (layer_out, kv_pages)


def solution(mesh):
    placed = (
        P(("req", "exp"), None),
        P(("req", "exp"), None),
        P(("req", "exp"), None),
        P(("req", "exp"), None),
        P("req"),
        P(),
        P(),
        P(),
        P(("req", "exp"), None),
        P(("req", "exp"), None),
        P(),
        P(),
        P(("req", "exp"), None, None),
        P(("req", "exp"), None, None),
    )
    return jax.shard_map(
        on_device,
        mesh=mesh,
        in_specs=placed,
        out_specs=(P(("req", "exp"), None), P("req", None, None, "exp")),
        check_vma=False,
    )
```

```python
import functools

import jax
import jax.numpy as jnp
from jax import lax
from jax.experimental import pallas as pl
from jax.experimental.pallas import tpu as pltpu
from jax.sharding import PartitionSpec as P

HEAD = 128
PAGE = 128

rope_base = 10000.0
norm_eps = 1e-06
masked_score = -1e30
CHUNK_ROWS = 2048


def turn(block, cosine, sines):
    wide = block.astype(jnp.float32)
    return (wide * cosine + pltpu.roll(wide, HEAD // 2, 1) * sines).astype(jnp.bfloat16)


def turn_keys_kernel(key_ref, value_ref, cos_ref, sin_ref, out_ref):
    width = key_ref.shape[1]
    cosine, sines = cos_ref[...], sin_ref[...]
    for start in range(0, width, HEAD):
        out_ref[:, start : start + HEAD] = turn(
            key_ref[:, start : start + HEAD], cosine, sines
        )
    out_ref[:, width:] = value_ref[...]


def turn_keys(keys, values, cosine, sines):
    rows, width = keys.shape
    return pl.pallas_call(
        turn_keys_kernel,
        out_shape=jax.ShapeDtypeStruct((rows, 2 * width), jnp.bfloat16),
        compiler_params=pltpu.CompilerParams(vmem_limit_bytes=32 << 20),
        name="turn_keys",
    )(keys, values, cosine, sines)


def attention_kernel(query_ref, key_ref, value_ref, cos_ref, sin_ref, mine_ref, all_ref, out_ref):
    cosine, sines = cos_ref[...], sin_ref[...]
    same = mine_ref[...] == all_ref[...]
    for start in range(0, query_ref.shape[1], HEAD):
        cols = slice(start, start + HEAD)
        query = turn(query_ref[:, cols], cosine, sines)
        scores = lax.dot_general(
            query, key_ref[:, cols], (((1,), (1,)), ((), ())), preferred_element_type=jnp.float32
        ) * HEAD ** (-0.5)
        scores = jnp.where(same, scores, masked_score)
        weights = jnp.where(same, jnp.exp(scores - jnp.max(scores, axis=1, keepdims=True)), 0.0)
        totals = jnp.sum(weights, axis=1, keepdims=True)
        mixed = jnp.dot(
            weights.astype(jnp.bfloat16), value_ref[:, cols], preferred_element_type=jnp.float32
        )
        out_ref[:, cols] = (mixed / totals).astype(jnp.bfloat16)


def attend(queries, keys_values, cosine, sines, my_segments, segments):
    rows, width = queries.shape
    all_rows = keys_values.shape[0]
    step = 512
    steps = width // step
    return pl.pallas_call(
        attention_kernel,
        grid=(steps,),
        in_specs=[
            pl.BlockSpec((rows, step), lambda i: (0, i)),
            pl.BlockSpec((all_rows, step), lambda i: (0, i)),
            pl.BlockSpec((all_rows, step), lambda i: (0, i + steps)),
            pl.BlockSpec((rows, HEAD), lambda i: (0, 0)),
            pl.BlockSpec((rows, HEAD), lambda i: (0, 0)),
            pl.BlockSpec((rows, 1), lambda i: (0, 0)),
            pl.BlockSpec((1, all_rows), lambda i: (0, 0)),
        ],
        out_specs=pl.BlockSpec((rows, step), lambda i: (0, i)),
        out_shape=jax.ShapeDtypeStruct((rows, width), jnp.bfloat16),
        compiler_params=pltpu.CompilerParams(vmem_limit_bytes=32 << 20),
        name="attend",
    )(queries, keys_values, keys_values, cosine, sines, my_segments[:, None], segments[None, :])


def pack_kernel(index_ref, key_ref, value_ref, out_ref):
    out_ref[0, 0] = key_ref[0]
    out_ref[0, 1] = value_ref[0]


def pack_pages(pages, index, columns, member_count):
    count = index.shape[0] - 1
    return pl.pallas_call(
        pack_kernel,
        grid_spec=pltpu.PrefetchScalarGridSpec(
            num_scalar_prefetch=1,
            grid=(count,),
            in_specs=[
                pl.BlockSpec((1, PAGE, columns), lambda i, index: (index[i], 0, index[count])),
                pl.BlockSpec(
                    (1, PAGE, columns), lambda i, index: (index[i], 0, index[count] + member_count)
                ),
            ],
            out_specs=pl.BlockSpec((1, 2, PAGE, columns), lambda i, index: (i, 0, 0, 0)),
        ),
        out_shape=jax.ShapeDtypeStruct((count, 2, PAGE, columns), jnp.bfloat16),
        name="pack_pages",
    )(index, pages, pages)


def place_kernel(index_ref, in_ref, out_ref):
    out_ref[...] = in_ref[...]


def place_pages(incoming, index):
    block = (1,) + incoming.shape[1:]
    return pl.pallas_call(
        place_kernel,
        grid_spec=pltpu.PrefetchScalarGridSpec(
            num_scalar_prefetch=1,
            grid=index.shape,
            in_specs=[pl.BlockSpec(block, lambda i, index: (index[i], 0, 0, 0))],
            out_specs=pl.BlockSpec(block, lambda i, index: (i, 0, 0, 0)),
        ),
        out_shape=jax.ShapeDtypeStruct(index.shape + incoming.shape[1:], jnp.bfloat16),
        name="place_pages",
    )(index, incoming)


def expert_kernel(rows_ref, gate_ref, pick_ref, inner_ref, outer_ref, out_ref):
    gates = jnp.sum(gate_ref[...].astype(jnp.float32) * pick_ref[...], axis=1, keepdims=True)
    projected = jnp.dot(rows_ref[...], inner_ref[0], preferred_element_type=jnp.float32)
    half = projected.shape[1] // 2
    first = projected[:, :half]
    active = (first / (1.0 + jnp.exp(-first)) * projected[:, half:]).astype(jnp.bfloat16)
    out = jnp.dot(active, outer_ref[0], preferred_element_type=jnp.float32)
    out_ref[...] = (out * gates).astype(jnp.bfloat16)


def half_expert(rows, pick, inner, outer):
    count, width = rows.shape[0], inner.shape[1]
    extra = pick.shape[1]
    step = min(512, count)
    once = pl.Buffered(1)
    return pl.pallas_call(
        expert_kernel,
        grid=(count // step,),
        in_specs=[
            pl.BlockSpec((step, width), lambda i: (i, 0)),
            pl.BlockSpec((step, extra), lambda i: (i, width // extra)),
            pl.BlockSpec((1, extra), lambda i: (0, 0)),
            pl.BlockSpec(inner.shape, lambda i: (0, 0, 0), pipeline_mode=once),
            pl.BlockSpec(outer.shape, lambda i: (0, 0, 0), pipeline_mode=once),
        ],
        out_specs=pl.BlockSpec((step, width), lambda i: (i, 0)),
        out_shape=jax.ShapeDtypeStruct((count, width), jnp.bfloat16),
        compiler_params=pltpu.CompilerParams(vmem_limit_bytes=48 << 20),
        cost_estimate=pl.CostEstimate(
            flops=2 * count * width * (inner.shape[2] + outer.shape[1]),
            bytes_accessed=4 * count * width,
            transcendentals=0,
        ),
        name="half_expert",
    )(rows, rows, pick, inner, outer)


def halve(blocks, member, distance):
    groups, members, rows, width = blocks.shape
    pairs = blocks.reshape(groups, members // 2, 2, rows, width)
    bit = (member >> distance) % 2
    kept = lax.dynamic_index_in_dim(pairs, bit, 2, keepdims=False)
    handed = lax.dynamic_index_in_dim(pairs, 1 - bit, 2, keepdims=False)
    swaps = [(i, i ^ 1 << distance) for i in range(lax.axis_size("exp"))]
    received = lax.ppermute(handed, "exp", swaps)
    return (kept.astype(jnp.float32) + received.astype(jnp.float32)).astype(jnp.bfloat16)


def on_device(
    residual,
    query_vectors,
    key_vectors,
    value_vectors,
    segment_ids,
    prompt_lengths,
    request_groups,
    page_table,
    expert_ids,
    gate_weights,
    out_weight,
    norm_gain,
    expert_inner,
    expert_outer,
):
    tok_rows, model_width = residual.shape
    req_count = lax.axis_size("req")
    member_count = lax.axis_size("exp")
    device_count = req_count * member_count
    expert_count = device_count // 2
    group_rows = tok_rows * member_count
    page_count = group_rows // PAGE
    columns = model_width // member_count
    everyone = ("req", "exp")
    group = lax.axis_index("req")
    member = lax.axis_index("exp")
    expert = (group * member_count + member) // 2

    holds_request = (request_groups == group).astype(jnp.int32)
    my_lengths = jnp.sum(holds_request[:, None] * prompt_lengths, axis=0)
    my_pages = jnp.sum(holds_request[:, None] * page_table, axis=0)
    first_row = member * tok_rows
    my_segments = lax.dynamic_slice_in_dim(segment_ids, first_row, tok_rows, 0)
    prompt_index = jnp.arange(prompt_lengths.shape[1], dtype=jnp.int32)
    token_start = jnp.sum(
        jnp.where(prompt_index[None, :] < my_segments[:, None], my_lengths[None, :], 0), axis=1
    )
    positions = (first_row + jnp.arange(tok_rows, dtype=jnp.int32) - token_start).astype(
        jnp.float32
    )
    inverse = rope_base ** (-(2.0 * jnp.arange(HEAD // 2, dtype=jnp.float32)) / HEAD)
    angles = positions[:, None] * inverse[None, :]
    cosine, sines = jnp.cos(angles), jnp.sin(angles)
    cosine = jnp.concatenate([cosine, cosine], axis=1)
    sines = jnp.concatenate([-sines, sines], axis=1)

    mine = turn_keys(key_vectors, value_vectors, cosine, sines)
    keys_values = lax.all_gather(mine, "exp", axis=0, tiled=True)

    expert_range = jnp.arange(expert_count, dtype=jnp.int32)
    dense_gates = jnp.sum(
        jnp.where(expert_ids[:, :, None] == expert_range[None, None, :], gate_weights[:, :, None], 0.0),
        axis=1,
    )
    high = dense_gates.astype(jnp.bfloat16)
    low = (dense_gates - high.astype(jnp.float32)).astype(jnp.bfloat16)
    spare = jnp.zeros((tok_rows, -2 * expert_count % 128), jnp.bfloat16)
    gate_columns = jnp.concatenate([high, low, spare], axis=1)
    lanes = jnp.arange(gate_columns.shape[1], dtype=jnp.int32)[None, :]
    pick = ((lanes == expert) | (lanes == expert + expert_count)).astype(jnp.float32)

    group_range = jnp.arange(req_count, dtype=jnp.int32)
    page_range = jnp.arange(page_count, dtype=jnp.int32)
    owned = my_pages[None, :] // page_count == group_range[:, None]
    page_for_group = jnp.sum(jnp.where(owned, page_range[None, :], 0), axis=1)
    outgoing = pack_pages(
        keys_values.reshape(page_count, PAGE, 2 * model_width),
        jnp.concatenate([page_for_group, member[None]]).astype(jnp.int32),
        columns,
        member_count,
    )
    incoming = lax.all_to_all(outgoing, "req", split_axis=0, concat_axis=0, tiled=True)
    slot_ids = group * page_count + page_range
    holds_slot = jnp.any(page_table[None, :, :] == slot_ids[:, None, None], axis=2)
    source_of_slot = jnp.sum(jnp.where(holds_slot, request_groups[None, :], 0), axis=1)
    kv_pages = place_pages(incoming, source_of_slot.astype(jnp.int32))

    attention = attend(query_vectors, keys_values, cosine, sines, my_segments, segment_ids)
    hidden = residual.astype(jnp.float32) + jnp.dot(
        attention, out_weight, preferred_element_type=jnp.float32
    )
    normed = (
        hidden * lax.rsqrt(jnp.mean(hidden * hidden, axis=-1, keepdims=True) + norm_eps) * norm_gain
    ).astype(jnp.bfloat16)

    chunks = 2 if device_count * tok_rows <= 2 * CHUNK_ROWS else 4
    part = tok_rows // chunks
    payload = jnp.concatenate([normed, gate_columns], axis=1)
    sums = []
    for chunk in range(chunks):
        rows = slice(chunk * part, (chunk + 1) * part)
        gathered = lax.all_gather(payload[rows], everyone, axis=0, tiled=True)
        partial_out = half_expert(gathered, pick, expert_inner, expert_outer)
        left = partial_out.reshape(req_count, member_count, part, model_width)
        distance = 0
        while left.shape[1] > 1:
            left = halve(left, member, distance)
            distance += 1
        arrived = lax.all_to_all(left[:, 0], "req", split_axis=0, concat_axis=0, tiled=True)
        sums.append(hidden[rows] + jnp.sum(arrived.astype(jnp.float32), axis=0))
    layer_out = jnp.concatenate(sums, axis=0).astype(jnp.bfloat16)
    return (layer_out, kv_pages)


def solution(mesh):
    placed = (
        P(("req", "exp"), None),
        P(("req", "exp"), None),
        P(("req", "exp"), None),
        P(("req", "exp"), None),
        P("req"),
        P(),
        P(),
        P(),
        P(("req", "exp"), None),
        P(("req", "exp"), None),
        P(),
        P(),
        P(("req", "exp"), None, None),
        P(("req", "exp"), None, None),
    )
    return jax.shard_map(
        on_device,
        mesh=mesh,
        in_specs=placed,
        out_specs=(P(("req", "exp"), None), P("req", None, None, "exp")),
        check_vma=False,
    )
```
